32 devices in a mesh: groups: 2 (over x), morton: 16 (over z, y, core).
Axes of the slice: x: 2, y: 2, z: 4, core: 2. Of those that a mesh axis runs over, the one named last changes fastest.
Arguments:
- features: bfloat16 [64, 512, 128], P(('groups', 'morton')), parts along dimension 0, may hold values from -6 to 6
- cotangent: bfloat16 [64, 512, 128], P(('groups', 'morton')), parts along dimension 0, may hold values from -6 to 6
- coarse: bfloat16 [128, 512, 256], P(('groups', 'morton')), parts along dimension 0, may hold values from -6 to 6
- kernel: bfloat16 [27, 128, 128], replicated, may hold values from -0.109375 to 0.109375
- coarse_weight: bfloat16 [256, 128], replicated, may hold values from -0.375 to 0.375
- brick_links: int32 [64, 27], P(('groups', 'morton')), parts along dimension 0, may hold values from -1 to 31, as said below
- parent_slot: int32 [64], P(('groups', 'morton')), parts along dimension 0, may hold values from 0 to 508, as said below
Outputs:
- grad_input: bfloat16 [64, 512, 128], P(('groups', 'morton')), parts along dimension 0
- grad_kernel: float32 [54, 128, 128], P('groups'), parts along dimension 0
- grad_coarse_weight: float32 [512, 128], P('groups'), parts along dimension 0
The draws below stay inside these ranges and needn't reach their ends.
There are 2 independent parts, one for each index of `groups`. The reference program is written for one: setup_inputs(seed, part) draws one part's arguments, and reference() takes and returns one part's arrays. A program takes and returns all parts, laid end to end along the dimension named above; an argument that names none is the same for every part. Nothing has to cross between parts.
Inputs may be any that keep to these rules, and one draw needn't show every extreme that they name: `brick_links`: entries are -1 or a brick index; links are symmetric. An index outside b's Morton range of 2 bricks lies in the range just before it, at an offset with dz = -1, or just after it, at an offset with dz = 1. `parent_slot`: 8 p + o with o = 4 oz + 2 oy + ox; p // 4 equals b // 2.
All inputs are finite; a program needn't handle non-finite values.
Results may differ from the reference program's by a relative error of at most 0.001.
The reference program's roundings to bfloat16 on the way count: a program that leaves them out, or rounds other values in their place, can miss the bound.
Values may be sent and summed in bfloat16 or wider, within the bound.
A program may use at most 64 MiB of HBM per device.

```python
import jax
import jax.numpy as jnp
from jax import lax

C = 128
CC = 256
LAY_DEV = 2
OCC = 1
BRICKS_PER_RANGE = 2
NBRICK = 32
NCOARSE = 64
N_MORTON = 16


def geometry(key):
    layers = LAY_DEV * N_MORTON
    keys = jax.random.split(key, layers + 2)
    orders = jax.vmap(lambda sub: jax.random.permutation(sub, 9))(keys[:layers])
    chosen = orders[:, :OCC].astype(jnp.int32)
    first_rest = jax.random.permutation(keys[layers], 8).astype(jnp.int32) + 1
    first_row = jnp.concatenate([jnp.zeros((1,), jnp.int32), first_rest[:OCC - 1]])
    last_rest = jax.random.permutation(keys[layers + 1], 8).astype(jnp.int32)
    last_row = jnp.concatenate([last_rest[:OCC - 1], jnp.full((1,), 8, jnp.int32)])
    chosen = chosen.at[0].set(first_row).at[layers - 1].set(last_row)
    chosen = jnp.sort(chosen, axis=1).astype(jnp.int32)
    layer_of = jnp.repeat(jnp.arange(layers, dtype=jnp.int32), OCC)
    place = chosen.reshape(-1)
    ident = jnp.arange(layers * OCC, dtype=jnp.int32)
    table = jnp.full((layers, 9), -1, jnp.int32).at[layer_of, place].set(ident)
    return (layer_of, place, table)


def draw_brick_links(key, part):
    layer_of, place, table = geometry(jax.random.fold_in(key, 11))
    layers = LAY_DEV * N_MORTON
    offsets = jnp.arange(27, dtype=jnp.int32)
    delta_z = offsets // 9 - 1
    delta_y = offsets // 3 % 3 - 1
    delta_x = offsets % 3 - 1
    layer_to = layer_of[:, None] + delta_z[None, :]
    row_to = (place // 3)[:, None] + delta_y[None, :]
    col_to = (place % 3)[:, None] + delta_x[None, :]
    inside = (layer_to >= 0) & (layer_to < layers) & (row_to >= 0) & (row_to < 3) & (col_to >= 0) & (col_to < 3)
    found = table[jnp.clip(layer_to, 0, layers - 1), jnp.clip(row_to, 0, 2) * 3 + jnp.clip(col_to, 0, 2)]
    return jnp.where(inside, found, -1).astype(jnp.int32)


def draw_parent_slot(key, part):
    layer_of, place, table = geometry(jax.random.fold_in(key, 11))
    row_at = place // 3
    col_at = place % 3
    parent = layer_of // 2 * 4 + row_at // 2 * 2 + col_at // 2
    octant = layer_of % 2 * 4 + row_at % 2 * 2 + col_at % 2
    return (parent * 8 + octant).astype(jnp.int32)


def level_of(own_key, dims, cuts, low, top_value):
    gain = 1.0
    for axis_at, parts in cuts:
        steps = jax.random.uniform(jax.random.fold_in(jax.random.fold_in(own_key, 6), axis_at), (parts,), jnp.float32, low / len(cuts), top_value / len(cuts))
        gain = gain * jnp.repeat(jnp.exp(steps), dims[axis_at] // parts).reshape((-1,) + (1,) * (len(dims) - 1 - axis_at))
    return gain


def scatter_about(key, extent, scale, limit, cuts=(), kind=jnp.bfloat16):
    level = level_of(key, extent, cuts, -0.22, 0.18) if cuts else 1.0
    entries = jax.random.normal(key, extent, jnp.float32) * scale * level
    return jnp.minimum(jnp.maximum(entries, -limit), limit).astype(kind)


def setup_inputs(seed: int = 0, part: int = 0) -> dict:
    key_list = jax.random.split(jax.random.key(seed), 8)
    part_keys = jax.random.split(jax.random.fold_in(key_list[7], part), 8)
    features = scatter_about(part_keys[0], (NBRICK, 512, C), 1.0, 6.0, ((0, 16),))
    cotangent = scatter_about(part_keys[1], (NBRICK, 512, C), 1.0, 6.0, ((0, 16),))
    coarse = scatter_about(part_keys[2], (NCOARSE, 512, CC), 1.0, 6.0, ((0, 16),))
    kernel = scatter_about(key_list[3], (27, C, C), (27 * C) ** -0.5, 0.109375)
    coarse_weight = scatter_about(key_list[4], (CC, C), CC ** -0.5, 0.375)
    brick_links = draw_brick_links(jax.random.fold_in(jax.random.fold_in(key_list[7], part), 71), part)
    parent_slot = draw_parent_slot(jax.random.fold_in(jax.random.fold_in(key_list[7], part), 71), part)
    return {"features": features, "cotangent": cotangent, "coarse": coarse, "kernel": kernel, "coarse_weight": coarse_weight, "brick_links": brick_links, "parent_slot": parent_slot}


SPANS = ((7, 8), (0, 8), (0, 1))


def build_padded(source, positions):
    planes = []
    for z_off in range(3):
        rows_list = []
        for y_off in range(3):
            pieces = []
            for x_off in range(3):
                zlo, zhi = SPANS[z_off]
                ylo, yhi = SPANS[y_off]
                xlo, xhi = SPANS[x_off]
                slab = source[:, zlo:zhi, ylo:yhi, xlo:xhi, :]
                pieces.append(slab[positions[:, z_off * 9 + y_off * 3 + x_off]])
            rows_list.append(jnp.concatenate(pieces, axis=3))
        planes.append(jnp.concatenate(rows_list, axis=2))
    return jnp.concatenate(planes, axis=1)


def convolve(padded, kernel):
    channels = kernel.shape[-1]
    grouped = kernel.reshape(9, 3 * channels, channels)
    summed = jnp.zeros((padded.shape[0] * 512, channels), jnp.float32)
    for z_off in range(3):
        for y_off in range(3):
            window = jnp.concatenate([padded[:, z_off:z_off + 8, y_off:y_off + 8, x_off:x_off + 8, :] for x_off in range(3)], axis=-1)
            summed = summed + jnp.dot(window.reshape(-1, 3 * channels), grouped[z_off * 3 + y_off], preferred_element_type=jnp.float32)
    return summed


def convolve_back(padded, kernel):
    channels = kernel.shape[-1]
    flipped = jnp.swapaxes(kernel, 1, 2).reshape(9, 3 * channels, channels)
    summed = jnp.zeros((padded.shape[0] * 512, channels), jnp.float32)
    for z_off in range(3):
        for y_off in range(3):
            window = jnp.concatenate([padded[:, 2 - z_off:10 - z_off, 2 - y_off:10 - y_off, 2 - x_off:10 - x_off, :] for x_off in range(3)], axis=-1)
            summed = summed + jnp.dot(window.reshape(-1, 3 * channels), flipped[z_off * 3 + y_off], preferred_element_type=jnp.float32)
    return summed


def weight_terms(padded, output_gradient):
    channels = output_gradient.shape[-1]
    pieces = []
    for z_off in range(3):
        for y_off in range(3):
            window = jnp.concatenate([padded[:, z_off:z_off + 8, y_off:y_off + 8, x_off:x_off + 8, :] for x_off in range(3)], axis=-1)
            term = lax.dot_general(window.reshape(-1, 3 * channels), output_gradient, (((0,), (0,)), ((), ())), preferred_element_type=jnp.float32)
            pieces.append(term.reshape(3, channels, channels))
    return jnp.concatenate(pieces, axis=0)


def octant_layout(coarse):
    brick_list, cells, chans = coarse.shape
    shaped = coarse.reshape(brick_list, 2, 4, 2, 4, 2, 4, chans).transpose(0, 1, 3, 5, 2, 4, 6, 7)
    return shaped.reshape(brick_list * 8, 64, chans)


def upsample(brick_region):
    brick_list, cells, chans = brick_region.shape
    shaped = brick_region.reshape(brick_list, 4, 1, 4, 1, 4, 1, chans)
    return jnp.broadcast_to(shaped, (brick_list, 4, 2, 4, 2, 4, 2, chans)).reshape(brick_list * 512, chans)


def reduce_resolution(gradient_rows, brick_list):
    chans = gradient_rows.shape[-1]
    return gradient_rows.astype(jnp.float32).reshape(brick_list, 4, 2, 4, 2, 4, 2, chans).sum(axis=(2, 4, 6)).reshape(brick_list * 64, chans)


def reference(features, cotangent, coarse, kernel, coarse_weight, brick_links, parent_slot):
    spare = jnp.zeros((1, 8, 8, 8, C), jnp.bfloat16)
    source = jnp.concatenate([features.reshape(NBRICK, 8, 8, 8, C), spare], axis=0)
    positions = jnp.where(brick_links < 0, NBRICK, brick_links).astype(jnp.int32)
    coarse_oct = octant_layout(coarse)
    projected = jnp.dot(coarse_oct.reshape(-1, CC), coarse_weight, preferred_element_type=jnp.float32).reshape(-1, 64, C)

    def forward_step(carry, block):
        start = (block * BRICKS_PER_RANGE).astype(jnp.int32)
        links = lax.dynamic_slice_in_dim(positions, start, BRICKS_PER_RANGE, 0)
        parents = lax.dynamic_slice_in_dim(parent_slot, start, BRICKS_PER_RANGE, 0)
        grads = lax.dynamic_slice_in_dim(cotangent, start, BRICKS_PER_RANGE, 0).reshape(-1, C).astype(jnp.float32)
        padded = build_padded(source, links)
        summed_in = convolve(padded, kernel) + upsample(projected[parents])
        sigmoid_at = jax.nn.sigmoid(summed_in)
        output_gradient = (grads * sigmoid_at * (1.0 + summed_in * (1.0 - sigmoid_at))).astype(jnp.bfloat16)
        kernel_term = weight_terms(padded, output_gradient)
        brick_region = coarse_oct[parents].reshape(-1, CC).astype(jnp.float32)
        coarse_contribution = lax.dot_general(brick_region, reduce_resolution(output_gradient, BRICKS_PER_RANGE), (((0,), (0,)), ((), ())), precision=lax.Precision.HIGHEST, preferred_element_type=jnp.float32)
        return (carry[0] + kernel_term, carry[1] + coarse_contribution), output_gradient.reshape(BRICKS_PER_RANGE, 8, 8, 8, C)

    init = (jnp.zeros((27, C, C), jnp.float32), jnp.zeros((CC, C), jnp.float32))
    blocks = jnp.arange(N_MORTON, dtype=jnp.int32)
    (kernel_sum, coarse_sum), slopes = lax.scan(forward_step, init, blocks)
    slope_source = jnp.concatenate([slopes.reshape(NBRICK, 8, 8, 8, C), spare], axis=0)

    def backward_block(block):
        start = (block * BRICKS_PER_RANGE).astype(jnp.int32)
        links = lax.dynamic_slice_in_dim(positions, start, BRICKS_PER_RANGE, 0)
        padded = build_padded(slope_source, links)
        return convolve_back(padded, kernel).astype(jnp.bfloat16)

    grad_rows = lax.map(backward_block, blocks)
    factor = (NBRICK * 512) ** -0.5
    return grad_rows.reshape(NBRICK, 512, C), kernel_sum * factor, coarse_sum * factor
```

```python
import functools

import jax
import jax.numpy as jnp
from jax import lax
from jax.experimental import pallas as pl
from jax.experimental.pallas import tpu as pltpu
from jax.sharding import PartitionSpec as P

MESH = pl.DeviceIdType.MESH
F32 = jnp.float32
BF16 = jnp.bfloat16
PIECES = 16
STAGES = 4
ORDERS = ((0, 1, 2, 3), (0, 2, 3, 1), (0, 1, 2, 3))


def bit(value, place):
    return (value // (1 << place)) % 2


def put_plane(rows_of, target, brick, plane):
    columns = [
        jnp.concatenate([rows_of(0, dx), rows_of(1, dx), rows_of(2, dx)], axis=0)
        for dx in range(3)
    ]
    at = lax.broadcasted_iota(jnp.int32, columns[1].shape, 1)
    shifted = (
        pltpu.roll(jnp.where(at == 7, columns[0], columns[1]), 1, 1),
        columns[1],
        pltpu.roll(jnp.where(at == 0, columns[2], columns[1]), 7, 1),
    )
    for dx in range(3):
        flat = shifted[dx].reshape(80, 128)
        for dy in range(3):
            lane = (3 * dy + dx) * 128
            target[brick, plane, :, lane : lane + 128] = flat[8 * dy : 8 * dy + 64].astype(BF16)


ROWS = (slice(7, 8), slice(0, 8), slice(0, 1))


def inner_planes(own, target, brick, index):
    @pl.loop(0, 8)
    def _(z):
        def rows_of(dy, dx):
            return own[index[9 + 3 * dy + dx], z, ROWS[dy]]

        put_plane(rows_of, target, brick, z + 1)


def edge_planes(top, bottom, target, brick, index):
    def rows_top(dy, dx):
        return top[index[3 * dy + dx], ROWS[dy]]

    def rows_bottom(dy, dx):
        return bottom[index[18 + 3 * dy + dx], ROWS[dy]]

    put_plane(rows_top, target, brick, 0)
    put_plane(rows_bottom, target, brick, 9)


def body(n, factor, links, parents, feat, cot, coarse, kern, cweight,
         gi_out, gk_out, gc_out,
         own, top, bottom, halo, slope, slope_halo, p9, s9, kt, up, slcat, *rest):
    accs, gaths = rest[0:3], rest[3:6]
    recvs = [rest[6 + 4 * c : 10 + 4 * c] for c in range(3)]
    extra_recvs = rest[18:21]
    send_sem, recv_sem, halo_send, halo_recv = rest[21:25]
    bricks = feat.shape[0]
    coarse_bricks = coarse.shape[0]
    me = lax.axis_index("morton")
    group = lax.axis_index("groups")
    after, before = (me + 1) % n, (me + n - 1) % n
    bits = n.bit_length() - 1
    partners = [me + (1 - 2 * bit(me, b)) * (1 << b) for b in range(bits)]

    barrier = pltpu.get_barrier_semaphore()
    for other in [after, before] + partners:
        pl.semaphore_signal(barrier, inc=1, device_id=(group, other), device_id_type=MESH)
    pl.semaphore_wait(barrier, 2 + bits)

    def send(source, dest, other, s_sem, r_sem):
        copy = pltpu.make_async_remote_copy(
            src_ref=source, dst_ref=dest, send_sem=s_sem, recv_sem=r_sem,
            device_id=(group, other), device_id_type=MESH,
        )
        copy.start()
        return copy

    copies = []

    def exchange_halo(source, dest, which):
        pair = [
            send(source.at[:, pl.ds(448, 64)], dest.at[0], after,
                 halo_send.at[which, 0], halo_recv.at[which, 0]),
            send(source.at[:, pl.ds(0, 64)], dest.at[1], before,
                 halo_send.at[which, 1], halo_recv.at[which, 1]),
        ]
        copies.extend(pair)
        return pair

    def take_halo(pair, dest):
        for side, copy in enumerate(pair):
            copy.wait_recv()
        for b in range(bricks):
            top[b] = dest[0, b].astype(F32).reshape(8, 8, 128)
            bottom[bricks + b] = dest[1, b].astype(F32).reshape(8, 8, 128)

    def set_own(b, cells):
        own[b] = cells
        top[bricks + b] = cells[7]
        bottom[b] = cells[0]

    pair = exchange_halo(feat, halo, 0)

    index = []
    for b in range(bricks):
        row = []
        for o in range(27):
            link = links[b, o]
            if o < 9:
                spot, spare = link - (me - 1) * bricks, 2 * bricks
            elif o < 18:
                spot, spare = link - me * bricks, bricks
            else:
                spot, spare = link - me * bricks, 2 * bricks
            row.append(jnp.where(link < 0, spare, jnp.clip(spot, 0, spare)))
        index.append(row)

    own[bricks] = jnp.zeros((8, 8, 8, 128), F32)
    top[2 * bricks] = jnp.zeros((8, 8, 128), F32)
    bottom[2 * bricks] = jnp.zeros((8, 8, 128), F32)
    for b in range(bricks):
        set_own(b, feat[b].astype(F32).reshape(8, 8, 8, 128))
    for b in range(bricks):
        inner_planes(own, p9, b, index[b])

    row_at = lax.broadcasted_iota(jnp.int32, (64, 64), 0)
    col_at = lax.broadcasted_iota(jnp.int32, (64, 64), 1)
    for b in range(bricks):
        slot = parents[b]
        octant = slot % 8
        parent = jnp.clip(slot // 8 - me * coarse_bricks, 0, coarse_bricks - 1)
        oz, oy, ox = octant // 4, (octant // 2) % 2, octant % 2
        wanted = (4 * oy + row_at // 16) * 8 + 4 * ox + (row_at % 8) // 2
        pick = jnp.where(col_at == wanted, 1.0, 0.0).astype(BF16)
        for zc in range(4):
            cells = coarse[parent, 4 * oz + zc]
            spread = jnp.dot(pick, cells, preferred_element_type=F32).astype(BF16)
            up[b, 2 * zc] = spread
            up[b, 2 * zc + 1] = spread

    for o in range(27):
        lane = (o % 9) * 128
        mirror = 26 - o
        kt[o // 9, :, lane : lane + 128] = kern[mirror // 9, (mirror % 9) * 128 : (mirror % 9) * 128 + 128, :]

    blank = jnp.zeros((64, 128), BF16)
    for b in range(bricks):
        for dz in range(3):
            for plane in list(range(dz)) + list(range(8 + dz, 10)):
                slcat[b, plane, :, dz * 128 : dz * 128 + 128] = blank

    take_halo(pair, halo)
    for b in range(bricks):
        edge_planes(top, bottom, p9, b, index[b])

    for b in range(bricks):
        total = jnp.dot(up[b].reshape(512, 256), cweight[...], preferred_element_type=F32)
        for dz in range(3):
            total = total + jnp.dot(
                p9[b, dz : dz + 8].reshape(512, 1152), kern[dz], preferred_element_type=F32
            )
        gate = jax.nn.sigmoid(total)
        grads = cot[b].astype(F32)
        value = (grads * gate * (1.0 + total * (1.0 - gate))).astype(BF16)
        slope[b] = value
        for dz in range(3):
            slcat[b, dz : dz + 8, :, dz * 128 : dz * 128 + 128] = value.reshape(8, 64, 128)

    slope_pair = exchange_halo(slope, slope_halo, 1)

    def reduce_chunk(c):
        order = ORDERS[c]
        acc, gath, recv, sem = accs[c], gaths[c], recvs[c], 0
        digits = [bit(me, b) for b in order]
        bases = [0]
        for k in range(STAGES):
            bases.append(bases[k] + digits[k] * (PIECES >> (k + 1)))
        for k in range(STAGES):
            half = PIECES >> (k + 1)
            away = bases[k] + (1 - digits[k]) * half
            copy = send(acc.at[pl.ds(away, half)], recv[k], partners[order[k]],
                        send_sem.at[c, sem], recv_sem.at[c, sem])
            copies.append(copy)
            sem += 1
            yield
            copy.wait_recv()
            acc[pl.ds(bases[k + 1], half)] = acc[pl.ds(bases[k + 1], half)] + recv[k][...]
        mine = bases[STAGES]
        for e in range(STAGES, bits):
            copy = send(acc.at[pl.ds(mine, 1)], extra_recvs[c].at[pl.ds(e - STAGES, 1)],
                        partners[e], send_sem.at[c, sem], recv_sem.at[c, sem])
            sem += 1
            yield
            copy.wait()
            acc[pl.ds(mine, 1)] = acc[pl.ds(mine, 1)] + extra_recvs[c][pl.ds(e - STAGES, 1)]
        gath[pl.ds(mine, 1)] = acc[pl.ds(mine, 1)] * factor
        for k in reversed(range(STAGES)):
            half = PIECES >> (k + 1)
            span = pl.ds(bases[k + 1], half)
            copy = send(gath.at[span], gath.at[span], partners[order[k]],
                        send_sem.at[c, sem], recv_sem.at[c, sem])
            copies.append(copy)
            sem += 1
            yield
            copy.wait_recv()
        total = gath[:, :72, :].reshape(9, 128, 128)
        for dz in range(3):
            for dx in range(3):
                gk_out[9 * dz + 3 * c + dx] = total[3 * dz + dx]
        if c == 2:
            gc_out[...] = gath[:, 72:, :].reshape(256, 128)

    running = []

    def advance():
        for chunk in list(running):
            if next(chunk, "end") == "end":
                running.remove(chunk)

    contract_rows = (((0,), (0,)), ((), ()))
    contract_lanes = (((1,), (1,)), ((), ()))
    wide = slcat[...].reshape(bricks * 640, 384)
    for dy in range(3):
        term = lax.dot_general(
            p9[:, :, :, dy * 384 : dy * 384 + 384].reshape(bricks * 640, 384), wide,
            contract_rows, preferred_element_type=F32,
        )
        stacked = jnp.concatenate([term[:, dz * 128 : dz * 128 + 128] for dz in range(3)], axis=0)
        accs[dy][:, :72, :] = stacked.reshape(PIECES, 72, 128)
        if dy == 2:
            term = lax.dot_general(
                up[...].reshape(bricks * 512, 256), slope[...].reshape(bricks * 512, 128),
                contract_rows, preferred_element_type=F32,
            )
            accs[2][:, 72:, :] = term.reshape(PIECES, 16, 128)
        running.append(reduce_chunk(dy))
        next(running[-1])

    for b in range(bricks):
        set_own(b, slope[b].astype(F32).reshape(8, 8, 8, 128))
    for b in range(bricks):
        inner_planes(own, s9, b, index[b])
        advance()
    take_halo(slope_pair, slope_halo)
    for b in range(bricks):
        edge_planes(top, bottom, s9, b, index[b])
    for b in range(bricks):
        total = jnp.zeros((512, 128), F32)
        for dz in range(3):
            total = total + lax.dot_general(
                s9[b, dz : dz + 8].reshape(512, 1152), kt[dz], contract_lanes,
                preferred_element_type=F32,
            )
        gi_out[b] = total.astype(BF16)
        advance()
    while running:
        advance()
    for copy in copies:
        copy.wait_send()


def local(n, features, cotangent, coarse, kernel, coarse_weight, brick_links, parent_slot):
    bricks = features.shape[0]
    bits = n.bit_length() - 1
    factor = (bricks * 512 * n) ** (-0.5)
    heights = (72, 72, 88)
    vmem = pltpu.VMEM
    scratch = [
        vmem((bricks + 1, 8, 8, 8, 128), F32),
        vmem((2 * bricks + 1, 8, 8, 128), F32),
        vmem((2 * bricks + 1, 8, 8, 128), F32),
        vmem((2, bricks, 64, 128), BF16),
        vmem((bricks, 512, 128), BF16),
        vmem((2, bricks, 64, 128), BF16),
        vmem((bricks, 10, 64, 1152), BF16),
        vmem((bricks, 10, 64, 1152), BF16),
        vmem((3, 128, 1152), BF16),
        vmem((bricks, 8, 64, 256), BF16),
        vmem((bricks, 10, 64, 384), BF16),
    ]
    scratch += [vmem((PIECES, h, 128), F32) for h in heights]
    scratch += [vmem((PIECES, h, 128), F32) for h in heights]
    for h in heights:
        scratch += [vmem((PIECES >> (k + 1), h, 128), F32) for k in range(STAGES)]
    scratch += [vmem((max(bits - STAGES, 1), h, 128), F32) for h in heights]
    steps = STAGES + bits
    dma = pltpu.SemaphoreType.DMA
    scratch += [dma((3, steps)), dma((3, steps)), dma((2, 2)), dma((2, 2))]
    in_vmem = pl.BlockSpec(memory_space=pltpu.VMEM)
    in_smem = pl.BlockSpec(memory_space=pltpu.SMEM)
    return pl.pallas_call(
        functools.partial(body, n, factor),
        out_shape=(
            jax.ShapeDtypeStruct(features.shape, BF16),
            jax.ShapeDtypeStruct((27, 128, 128), F32),
            jax.ShapeDtypeStruct((256, 128), F32),
        ),
        in_specs=[in_smem, in_smem] + [in_vmem] * 5,
        out_specs=(in_vmem, in_vmem, in_vmem),
        scratch_shapes=scratch,
        compiler_params=pltpu.CompilerParams(
            collective_id=0, has_side_effects=True, vmem_limit_bytes=48 * 1024 * 1024
        ),
        cost_estimate=pl.CostEstimate(flops=3_000_000_000, bytes_accessed=8_000_000, transcendentals=0),
    )(brick_links, parent_slot, features, cotangent,
      coarse.reshape(coarse.shape[0], 8, 64, 256), kernel.reshape(3, 1152, 128), coarse_weight)


def solution(mesh):
    return jax.shard_map(
        functools.partial(local, mesh.shape["morton"]),
        mesh=mesh,
        in_specs=(
            P(("groups", "morton"), None, None),
            P(("groups", "morton"), None, None),
            P(("groups", "morton"), None, None),
            P(),
            P(),
            P(("groups", "morton"), None),
            P(("groups", "morton")),
        ),
        out_specs=(P(("groups", "morton"), None, None), P("groups", None, None), P("groups", None)),
        check_vma=False,
    )
```

```python
import functools

import jax
import jax.numpy as jnp
from jax import lax
from jax.experimental import pallas as pl
from jax.experimental.pallas import tpu as pltpu
from jax.sharding import PartitionSpec as P

MESH = pl.DeviceIdType.MESH
F32 = jnp.float32
BF16 = jnp.bfloat16
PIECES = 16
STAGES = 4
ORDERS = ((0, 1, 2, 3), (0, 2, 3, 1), (0, 1, 2, 3))
LEVELS = 32000.0
TINY = 2.0**-100


def encode(values):
    pieces = values.shape[0]
    peak = jnp.maximum(jnp.max(jnp.abs(values), axis=1, keepdims=True), TINY)
    power = jnp.ceil(jnp.log2(peak))
    scaled = values * (jnp.exp2(-power) * LEVELS)
    both = jnp.concatenate([scaled, jnp.broadcast_to(power, (pieces, 8, 128))], axis=1)
    return jnp.floor(both + 0.5).astype(jnp.int32).astype(jnp.int16)


def decode(codes):
    rows = codes.shape[1] - 8
    both = codes.astype(jnp.int32).astype(F32)
    return both[:, :rows] * (jnp.exp2(both[:, rows : rows + 1]) * (1.0 / LEVELS))


def bit(value, place):
    return (value // (1 << place)) % 2


def put_plane(rows_of, target, brick, plane):
    columns = [
        jnp.concatenate([rows_of(0, dx), rows_of(1, dx), rows_of(2, dx)], axis=0)
        for dx in range(3)
    ]
    at = lax.broadcasted_iota(jnp.int32, columns[1].shape, 1)
    shifted = (
        pltpu.roll(jnp.where(at == 7, columns[0], columns[1]), 1, 1),
        columns[1],
        pltpu.roll(jnp.where(at == 0, columns[2], columns[1]), 7, 1),
    )
    for dx in range(3):
        flat = shifted[dx].reshape(80, 128)
        for dy in range(3):
            lane = (3 * dy + dx) * 128
            target[brick, plane, :, lane : lane + 128] = flat[8 * dy : 8 * dy + 64].astype(BF16)


ROWS = (slice(7, 8), slice(0, 8), slice(0, 1))


def inner_planes(own, target, brick, index):
    @pl.loop(0, 8)
    def _(z):
        def rows_of(dy, dx):
            return own[index[9 + 3 * dy + dx], z, ROWS[dy]]

        put_plane(rows_of, target, brick, z + 1)


def edge_planes(top, bottom, target, brick, index):
    def rows_top(dy, dx):
        return top[index[3 * dy + dx], ROWS[dy]]

    def rows_bottom(dy, dx):
        return bottom[index[18 + 3 * dy + dx], ROWS[dy]]

    put_plane(rows_top, target, brick, 0)
    put_plane(rows_bottom, target, brick, 9)


def body(n, factor, links_in, parents_in, feat_in, cot_in, coarse_in, kern_in, cweight_in,
         gi_out, gath_a, gath_b, gath_c,
         links, parents, feat, cot, coarse, kern, cweight, load_sem,
         own, top, bottom, halo, slope, slope_halo, p9, s9, kt, up, slcat, *rest):
    accs, codes, gaths = rest[0:3], rest[3:6], (gath_a, gath_b, gath_c)
    recvs = [rest[6 + 4 * c : 10 + 4 * c] for c in range(3)]
    extra_recvs = rest[18:21]
    send_sem, recv_sem, halo_send, halo_recv = rest[21:25]
    bricks = feat.shape[0]
    coarse_bricks = coarse.shape[0]
    me = lax.axis_index("morton")
    group = lax.axis_index("groups")
    after, before = (me + 1) % n, (me + n - 1) % n
    bits = n.bit_length() - 1
    partners = [me + (1 - 2 * bit(me, b)) * (1 << b) for b in range(bits)]

    sources = (links_in, parents_in, feat_in, kern_in, coarse_in, cweight_in, cot_in)
    places = (links, parents, feat, kern, coarse, cweight, cot)
    loads = [
        pltpu.make_async_copy(source, place, load_sem.at[i])
        for i, (source, place) in enumerate(zip(sources, places))
    ]
    for load in loads:
        load.start()

    barrier = pltpu.get_barrier_semaphore()
    for other in [after, before] + partners:
        pl.semaphore_signal(barrier, inc=1, device_id=(group, other), device_id_type=MESH)
    pl.semaphore_wait(barrier, 2 + bits)

    def send(source, dest, other, s_sem, r_sem):
        copy = pltpu.make_async_remote_copy(
            src_ref=source, dst_ref=dest, send_sem=s_sem, recv_sem=r_sem,
            device_id=(group, other), device_id_type=MESH,
        )
        copy.start()
        return copy

    copies = []

    def exchange_halo(source, dest, which):
        pair = [
            send(source.at[:, pl.ds(448, 64)], dest.at[0], after,
                 halo_send.at[which, 0], halo_recv.at[which, 0]),
            send(source.at[:, pl.ds(0, 64)], dest.at[1], before,
                 halo_send.at[which, 1], halo_recv.at[which, 1]),
        ]
        copies.extend(pair)
        return pair

    def take_halo(pair, dest):
        for side, copy in enumerate(pair):
            copy.wait_recv()
        for b in range(bricks):
            top[b] = dest[0, b].astype(F32).reshape(8, 8, 128)
            bottom[bricks + b] = dest[1, b].astype(F32).reshape(8, 8, 128)

    def set_own(b, cells):
        own[b] = cells
        top[bricks + b] = cells[7]
        bottom[b] = cells[0]

    pair = exchange_halo(feat_in, halo, 0)
    for load in loads[:3]:
        load.wait()

    index = []
    for b in range(bricks):
        row = []
        for o in range(27):
            link = links[b, o]
            if o < 9:
                spot, spare = link - (me - 1) * bricks, 2 * bricks
            elif o < 18:
                spot, spare = link - me * bricks, bricks
            else:
                spot, spare = link - me * bricks, 2 * bricks
            row.append(jnp.where(link < 0, spare, jnp.clip(spot, 0, spare)))
        index.append(row)

    own[bricks] = jnp.zeros((8, 8, 8, 128), F32)
    top[2 * bricks] = jnp.zeros((8, 8, 128), F32)
    bottom[2 * bricks] = jnp.zeros((8, 8, 128), F32)
    for b in range(bricks):
        set_own(b, feat[b].astype(F32).reshape(8, 8, 8, 128))
    for b in range(bricks):
        inner_planes(own, p9, b, index[b])

    for load in loads[3:]:
        load.wait()
    row_at = lax.broadcasted_iota(jnp.int32, (64, 64), 0)
    col_at = lax.broadcasted_iota(jnp.int32, (64, 64), 1)
    for b in range(bricks):
        slot = parents[b]
        octant = slot % 8
        parent = jnp.clip(slot // 8 - me * coarse_bricks, 0, coarse_bricks - 1)
        oz, oy, ox = octant // 4, (octant // 2) % 2, octant % 2
        wanted = (4 * oy + row_at // 16) * 8 + 4 * ox + (row_at % 8) // 2
        pick = jnp.where(col_at == wanted, 1.0, 0.0).astype(BF16)
        for zc in range(4):
            cells = coarse[parent, 4 * oz + zc]
            spread = jnp.dot(pick, cells, preferred_element_type=F32).astype(BF16)
            up[b, 2 * zc] = spread
            up[b, 2 * zc + 1] = spread

    for o in range(27):
        lane = (o % 9) * 128
        mirror = 26 - o
        kt[o // 9, :, lane : lane + 128] = kern[mirror // 9, (mirror % 9) * 128 : (mirror % 9) * 128 + 128, :]

    blank = jnp.zeros((64, 128), BF16)
    for b in range(bricks):
        for dz in range(3):
            for plane in list(range(dz)) + list(range(8 + dz, 10)):
                slcat[b, plane, :, dz * 128 : dz * 128 + 128] = blank

    take_halo(pair, halo)
    for b in range(bricks):
        edge_planes(top, bottom, p9, b, index[b])

    for b in range(bricks):
        total = jnp.dot(up[b].reshape(512, 256), cweight[...], preferred_element_type=F32)
        for dz in range(3):
            total = total + jnp.dot(
                p9[b, dz : dz + 8].reshape(512, 1152), kern[dz], preferred_element_type=F32
            )
        gate = jax.nn.sigmoid(total)
        grads = cot[b].astype(F32)
        value = (grads * gate * (1.0 + total * (1.0 - gate))).astype(BF16)
        slope[b] = value
        for dz in range(3):
            slcat[b, dz : dz + 8, :, dz * 128 : dz * 128 + 128] = value.reshape(8, 64, 128)

    slope_pair = exchange_halo(slope, slope_halo, 1)

    def reduce_chunk(c):
        order = ORDERS[c]
        acc, gath, recv, sem = accs[c], gaths[c], recvs[c], 0
        digits = [bit(me, b) for b in order]
        bases = [0]
        for k in range(STAGES):
            bases.append(bases[k] + digits[k] * (PIECES >> (k + 1)))
        for k in range(STAGES):
            half = PIECES >> (k + 1)
            away = bases[k] + (1 - digits[k]) * half
            if k == 0:
                source = acc.at[pl.ds(away, half)]
            else:
                source = codes[c].at[pl.ds(PIECES - 2 * half, half)]
                source[...] = encode(acc[pl.ds(away, half)])
            copy = send(source, recv[k], partners[order[k]],
                        send_sem.at[c, sem], recv_sem.at[c, sem])
            copies.append(copy)
            sem += 1
            yield
            copy.wait_recv()
            other = recv[k][...] if k == 0 else decode(recv[k][...])
            acc[pl.ds(bases[k + 1], half)] = acc[pl.ds(bases[k + 1], half)] + other
        mine = bases[STAGES]
        for e in range(STAGES, bits):
            copy = send(acc.at[pl.ds(mine, 1)], extra_recvs[c].at[pl.ds(e - STAGES, 1)],
                        partners[e], send_sem.at[c, sem], recv_sem.at[c, sem])
            sem += 1
            yield
            copy.wait()
            acc[pl.ds(mine, 1)] = acc[pl.ds(mine, 1)] + extra_recvs[c][pl.ds(e - STAGES, 1)]
        gath[pl.ds(mine, 1)] = encode(acc[pl.ds(mine, 1)] * factor)
        for k in reversed(range(STAGES)):
            half = PIECES >> (k + 1)
            span = pl.ds(bases[k + 1], half)
            copy = send(gath.at[span], gath.at[span], partners[order[k]],
                        send_sem.at[c, sem], recv_sem.at[c, sem])
            copies.append(copy)
            sem += 1
            yield
            copy.wait_recv()

    running = []

    def advance():
        for chunk in list(running):
            if next(chunk, "end") == "end":
                running.remove(chunk)

    contract_rows = (((0,), (0,)), ((), ()))
    contract_lanes = (((1,), (1,)), ((), ()))
    wide = slcat[...].reshape(bricks * 640, 384)
    for dy in range(3):
        term = lax.dot_general(
            p9[:, :, :, dy * 384 : dy * 384 + 384].reshape(bricks * 640, 384), wide,
            contract_rows, preferred_element_type=F32,
        )
        stacked = jnp.concatenate([term[:, dz * 128 : dz * 128 + 128] for dz in range(3)], axis=0)
        accs[dy][:, :72, :] = stacked.reshape(PIECES, 72, 128)
        if dy == 2:
            term = lax.dot_general(
                up[...].reshape(bricks * 512, 256), slope[...].reshape(bricks * 512, 128),
                contract_rows, preferred_element_type=F32,
            )
            accs[2][:, 72:, :] = term.reshape(PIECES, 16, 128)
        running.append(reduce_chunk(dy))
        next(running[-1])

    for b in range(bricks):
        set_own(b, slope[b].astype(F32).reshape(8, 8, 8, 128))
    for b in range(bricks):
        inner_planes(own, s9, b, index[b])
        advance()
    take_halo(slope_pair, slope_halo)
    for b in range(bricks):
        edge_planes(top, bottom, s9, b, index[b])
    for b in range(bricks):
        total = jnp.zeros((512, 128), F32)
        for dz in range(3):
            total = total + lax.dot_general(
                s9[b, dz : dz + 8].reshape(512, 1152), kt[dz], contract_lanes,
                preferred_element_type=F32,
            )
        gi_out[b] = total.astype(BF16)
        advance()
    while running:
        advance()
    for copy in copies:
        copy.wait_send()


def finish(gi_in, gath_a, gath_b, gath_c, gi_out, gk_out, gc_out, gk, gc, sems):
    first = pltpu.make_async_copy(gi_in, gi_out, sems.at[0])
    first.start()
    copies = [first]
    for c, gath in enumerate((gath_a, gath_b, gath_c)):
        values = decode(gath[...])
        total = values[:, :72, :].reshape(3, 384, 128)
        for dz in range(3):
            gk[dz, c] = total[dz]
        copy = pltpu.make_async_copy(gk.at[:, c], gk_out.at[:, c], sems.at[1 + c])
        copy.start()
        copies.append(copy)
        if c == 2:
            gc[...] = values[:, 72:, :].reshape(256, 128)
    last = pltpu.make_async_copy(gc, gc_out, sems.at[4])
    last.start()
    for copy in copies + [last]:
        copy.wait()


def local(n, features, cotangent, coarse, kernel, coarse_weight, brick_links, parent_slot):
    bricks = features.shape[0]
    bits = n.bit_length() - 1
    factor = (bricks * 512 * n) ** (-0.5)
    heights = (72, 72, 88)
    vmem = pltpu.VMEM
    tall = coarse.shape[0]
    smem = pltpu.SMEM
    scratch = [
        smem(brick_links.shape, jnp.int32),
        smem(parent_slot.shape, jnp.int32),
        vmem((bricks, 512, 128), BF16),
        vmem((bricks, 512, 128), BF16),
        vmem((tall, 8, 64, 256), BF16),
        vmem((3, 1152, 128), BF16),
        vmem((256, 128), BF16),
        pltpu.SemaphoreType.DMA((7,)),
        vmem((bricks + 1, 8, 8, 8, 128), F32),
        vmem((2 * bricks + 1, 8, 8, 128), F32),
        vmem((2 * bricks + 1, 8, 8, 128), F32),
        vmem((2, bricks, 64, 128), BF16),
        vmem((bricks, 512, 128), BF16),
        vmem((2, bricks, 64, 128), BF16),
        vmem((bricks, 10, 64, 1152), BF16),
        vmem((bricks, 10, 64, 1152), BF16),
        vmem((3, 128, 1152), BF16),
        vmem((bricks, 8, 64, 256), BF16),
        vmem((bricks, 10, 64, 384), BF16),
    ]
    short = jnp.int16
    scratch += [vmem((PIECES, h, 128), F32) for h in heights]
    scratch += [vmem((PIECES, h + 8, 128), short) for h in heights]
    for h in heights:
        scratch += [vmem((PIECES // 2, h, 128), F32)]
        scratch += [vmem((PIECES >> (k + 1), h + 8, 128), short) for k in range(1, STAGES)]
    scratch += [vmem((max(bits - STAGES, 1), h, 128), F32) for h in heights]
    steps = STAGES + bits
    dma = pltpu.SemaphoreType.DMA
    scratch += [dma((3, steps)), dma((3, steps)), dma((2, 2)), dma((2, 2))]
    in_vmem = pl.BlockSpec(memory_space=pltpu.VMEM)
    in_hbm = pl.BlockSpec(memory_space=pltpu.HBM)
    grad, gath_a, gath_b, gath_c = pl.pallas_call(
        functools.partial(body, n, factor),
        out_shape=[jax.ShapeDtypeStruct(features.shape, BF16)]
        + [jax.ShapeDtypeStruct((PIECES, h + 8, 128), short) for h in heights],
        in_specs=[in_hbm] * 7,
        out_specs=[in_vmem] * 4,
        scratch_shapes=scratch,
        compiler_params=pltpu.CompilerParams(
            collective_id=0, has_side_effects=True, vmem_limit_bytes=40 * 1024 * 1024
        ),
        cost_estimate=pl.CostEstimate(flops=3_000_000_000, bytes_accessed=8_000_000, transcendentals=0),
    )(brick_links, parent_slot, features, cotangent,
      coarse.reshape(tall, 8, 64, 256), kernel.reshape(3, 1152, 128), coarse_weight)
    grad, grad_kernel, grad_coarse = pl.pallas_call(
        finish,
        out_shape=(
            jax.ShapeDtypeStruct(features.shape, BF16),
            jax.ShapeDtypeStruct((3, 3, 3 * 128, 128), F32),
            jax.ShapeDtypeStruct((256, 128), F32),
        ),
        in_specs=[in_vmem] * 4,
        out_specs=(in_hbm, in_hbm, in_hbm),
        scratch_shapes=[
            vmem((3, 3, 3 * 128, 128), F32), vmem((256, 128), F32), dma((5,)),
        ],
        compiler_params=pltpu.CompilerParams(vmem_limit_bytes=16 * 1024 * 1024),
    )(grad, gath_a, gath_b, gath_c)
    return grad, grad_kernel.reshape(27, 128, 128), grad_coarse


def solution(mesh):
    return jax.shard_map(
        functools.partial(local, mesh.shape["morton"]),
        mesh=mesh,
        in_specs=(
            P(("groups", "morton"), None, None),
            P(("groups", "morton"), None, None),
            P(("groups", "morton"), None, None),
            P(),
            P(),
            P(("groups", "morton"), None),
            P(("groups", "morton")),
        ),
        out_specs=(P(("groups", "morton"), None, None), P("groups", None, None), P("groups", None)),
        check_vma=False,
    )
```

```python
import functools

import jax
import jax.numpy as jnp
from jax import lax
from jax.experimental import pallas as pl
from jax.experimental.pallas import tpu as pltpu
from jax.sharding import PartitionSpec as P

MESH = pl.DeviceIdType.MESH
F32 = jnp.float32
BF16 = jnp.bfloat16
PIECES = 16
SPLIT_BITS = 4
ORDERS = (((0,), (1,), (2, 3)), ((0,), (2, 3), (1,)), ((0,), (1,), (2, 3)))
LEVELS = 32000.0
TINY = 2.0**-100


def encode(values):
    pieces = values.shape[0]
    peak = jnp.maximum(jnp.max(jnp.abs(values), axis=1, keepdims=True), TINY)
    power = jnp.ceil(jnp.log2(peak))
    scaled = values * (jnp.exp2(-power) * LEVELS)
    both = jnp.concatenate([scaled, jnp.broadcast_to(power, (pieces, 8, 128))], axis=1)
    return jnp.floor(both + 0.5).astype(jnp.int32).astype(jnp.int16)


def decode(codes):
    rows = codes.shape[1] - 8
    both = codes.astype(jnp.int32).astype(F32)
    return both[:, :rows] * (jnp.exp2(both[:, rows : rows + 1]) * (1.0 / LEVELS))


def bit(value, place):
    return (value // (1 << place)) % 2


def stage_parts(order):
    size, parts = PIECES, []
    for group in order:
        size >>= len(group)
        parts.append((size, (1 << len(group)) - 1))
    return parts


def put_plane(rows_of, target, brick, plane):
    columns = [
        jnp.concatenate([rows_of(0, dx), rows_of(1, dx), rows_of(2, dx)], axis=0)
        for dx in range(3)
    ]
    at = lax.broadcasted_iota(jnp.int32, columns[1].shape, 1)
    shifted = (
        pltpu.roll(jnp.where(at == 7, columns[0], columns[1]), 1, 1),
        columns[1],
        pltpu.roll(jnp.where(at == 0, columns[2], columns[1]), 7, 1),
    )
    for dx in range(3):
        flat = shifted[dx].reshape(80, 128)
        for dy in range(3):
            lane = (3 * dy + dx) * 128
            target[brick, plane, :, lane : lane + 128] = flat[8 * dy : 8 * dy + 64].astype(BF16)


ROWS = (slice(7, 8), slice(0, 8), slice(0, 1))


def inner_planes(own, target, brick, index):
    @pl.loop(0, 8)
    def _(z):
        def rows_of(dy, dx):
            return own[index[9 + 3 * dy + dx], z, ROWS[dy]]

        put_plane(rows_of, target, brick, z + 1)


def edge_planes(top, bottom, target, brick, index):
    def rows_top(dy, dx):
        return top[index[3 * dy + dx], ROWS[dy]]

    def rows_bottom(dy, dx):
        return bottom[index[18 + 3 * dy + dx], ROWS[dy]]

    put_plane(rows_top, target, brick, 0)
    put_plane(rows_bottom, target, brick, 9)


def body(n, factor, links_in, parents_in, feat_in, cot_in, coarse_in, kern_in, cweight_in,
         gi_out, gath_a, gath_b, gath_c,
         links, parents, feat, cot, coarse, kern, cweight, load_sem,
         own, top, bottom, halo, slope, slope_halo, p9, s9, kt, up, slcat, *rest):
    accs, codes, gaths = rest[0:3], rest[3:6], (gath_a, gath_b, gath_c)
    stages = len(ORDERS[0])
    recvs = [rest[6 + stages * c : 6 + stages * (c + 1)] for c in range(3)]
    extra_recvs = rest[6 + 3 * stages : 9 + 3 * stages]
    send_sem, recv_sem, halo_send, halo_recv = rest[9 + 3 * stages :]
    bricks = feat.shape[0]
    coarse_bricks = coarse.shape[0]
    me = lax.axis_index("morton")
    group = lax.axis_index("groups")
    after, before = (me + 1) % n, (me + n - 1) % n
    bits = n.bit_length() - 1

    def partner(places):
        other = me
        for b in places:
            other = other + (1 - 2 * bit(me, b)) * (1 << b)
        return other

    def toggles(group):
        return [
            [j for j in range(len(group)) if mask >> j & 1] for mask in range(1, 1 << len(group))
        ]

    partners = [
        partner([group[j] for j in chosen]) for group in ORDERS[0] for chosen in toggles(group)
    ] + [partner([b]) for b in range(SPLIT_BITS, bits)]

    sources = (links_in, parents_in, feat_in, kern_in, coarse_in, cweight_in, cot_in)
    places = (links, parents, feat, kern, coarse, cweight, cot)
    loads = [
        pltpu.make_async_copy(source, place, load_sem.at[i])
        for i, (source, place) in enumerate(zip(sources, places))
    ]
    for load in loads:
        load.start()

    barrier = pltpu.get_barrier_semaphore()
    for other in [after, before] + partners:
        pl.semaphore_signal(barrier, inc=1, device_id=(group, other), device_id_type=MESH)

    def send(source, dest, other, s_sem, r_sem):
        copy = pltpu.make_async_remote_copy(
            src_ref=source, dst_ref=dest, send_sem=s_sem, recv_sem=r_sem,
            device_id=(group, other), device_id_type=MESH,
        )
        copy.start()
        return copy

    copies = []

    def exchange_halo(source, dest, which):
        pair = [
            send(source.at[:, pl.ds(448, 64)], dest.at[0], after,
                 halo_send.at[which, 0], halo_recv.at[which, 0]),
            send(source.at[:, pl.ds(0, 64)], dest.at[1], before,
                 halo_send.at[which, 1], halo_recv.at[which, 1]),
        ]
        copies.extend(pair)
        return pair

    def take_halo(pair, dest):
        for side, copy in enumerate(pair):
            copy.wait_recv()
        for b in range(bricks):
            top[b] = dest[0, b].astype(F32).reshape(8, 8, 128)
            bottom[bricks + b] = dest[1, b].astype(F32).reshape(8, 8, 128)

    def set_own(b, cells):
        own[b] = cells
        top[bricks + b] = cells[7]
        bottom[b] = cells[0]

    for load in loads[:3]:
        load.wait()

    index = []
    for b in range(bricks):
        row = []
        for o in range(27):
            link = links[b, o]
            if o < 9:
                spot, spare = link - (me - 1) * bricks, 2 * bricks
            elif o < 18:
                spot, spare = link - me * bricks, bricks
            else:
                spot, spare = link - me * bricks, 2 * bricks
            row.append(jnp.where(link < 0, spare, jnp.clip(spot, 0, spare)))
        index.append(row)

    own[bricks] = jnp.zeros((8, 8, 8, 128), F32)
    top[2 * bricks] = jnp.zeros((8, 8, 128), F32)
    bottom[2 * bricks] = jnp.zeros((8, 8, 128), F32)
    for b in range(bricks):
        set_own(b, feat[b].astype(F32).reshape(8, 8, 8, 128))
    for b in range(bricks):
        inner_planes(own, p9, b, index[b])
    pl.semaphore_wait(barrier, 2 + len(partners))
    pair = exchange_halo(feat_in, halo, 0)

    for load in loads[3:]:
        load.wait()
    row_at = lax.broadcasted_iota(jnp.int32, (64, 64), 0)
    col_at = lax.broadcasted_iota(jnp.int32, (64, 64), 1)
    for b in range(bricks):
        slot = parents[b]
        octant = slot % 8
        parent = jnp.clip(slot // 8 - me * coarse_bricks, 0, coarse_bricks - 1)
        oz, oy, ox = octant // 4, (octant // 2) % 2, octant % 2
        wanted = (4 * oy + row_at // 16) * 8 + 4 * ox + (row_at % 8) // 2
        pick = jnp.where(col_at == wanted, 1.0, 0.0).astype(BF16)
        for zc in range(4):
            cells = coarse[parent, 4 * oz + zc]
            spread = jnp.dot(pick, cells, preferred_element_type=F32).astype(BF16)
            up[b, 2 * zc] = spread
            up[b, 2 * zc + 1] = spread

    for o in range(27):
        lane = (o % 9) * 128
        mirror = 26 - o
        kt[o // 9, :, lane : lane + 128] = kern[mirror // 9, (mirror % 9) * 128 : (mirror % 9) * 128 + 128, :]

    blank = jnp.zeros((64, 128), BF16)
    for b in range(bricks):
        for dz in range(3):
            for plane in list(range(dz)) + list(range(8 + dz, 10)):
                slcat[b, plane, :, dz * 128 : dz * 128 + 128] = blank

    take_halo(pair, halo)
    for b in range(bricks):
        edge_planes(top, bottom, p9, b, index[b])

    for b in range(bricks):
        total = jnp.dot(up[b].reshape(512, 256), cweight[...], preferred_element_type=F32)
        for dz in range(3):
            total = total + jnp.dot(
                p9[b, dz : dz + 8].reshape(512, 1152), kern[dz], preferred_element_type=F32
            )
        gate = jax.nn.sigmoid(total)
        grads = cot[b].astype(F32)
        value = (grads * gate * (1.0 + total * (1.0 - gate))).astype(BF16)
        slope[b] = value
        for dz in range(3):
            slcat[b, dz : dz + 8, :, dz * 128 : dz * 128 + 128] = value.reshape(8, 64, 128)

    slope_pair = exchange_halo(slope, slope_halo, 1)

    def reduce_chunk(c):
        order = ORDERS[c]
        acc, gath, recv, sem = accs[c], gaths[c], recvs[c], 0
        parts = stage_parts(order)
        digits = [
            sum(bit(me, b) * (1 << (len(group) - 1 - j)) for j, b in enumerate(group)) for group in order
        ]
        bases = [0]
        for digit, (size, _) in zip(digits, parts):
            bases.append(bases[-1] + digit * size)
        filled = 0
        for k, (group, (size, _)) in enumerate(zip(order, parts)):
            batch = []
            for slot, chosen in enumerate(toggles(group)):
                digit = digits[k]
                for j in chosen:
                    digit = digit + (1 - 2 * bit(me, group[j])) * (1 << (len(group) - 1 - j))
                source = acc.at[pl.ds(bases[k] + digit * size, size)]
                if k > 0:
                    coded = codes[c].at[pl.ds(filled, size)]
                    coded[...] = encode(source[...])
                    source = coded
                    filled += size
                batch.append(
                    send(source, recv[k].at[slot], partner([group[j] for j in chosen]),
                         send_sem.at[c, sem], recv_sem.at[c, sem])
                )
                sem += 1
            copies.extend(batch)
            yield
            span = pl.ds(bases[k + 1], size)
            total = acc[span]
            for slot, copy in enumerate(batch):
                copy.wait_recv()
                total = total + (recv[k][slot] if k == 0 else decode(recv[k][slot]))
            acc[span] = total
        mine = bases[-1]
        for e in range(SPLIT_BITS, bits):
            copy = send(acc.at[pl.ds(mine, 1)], extra_recvs[c].at[pl.ds(e - SPLIT_BITS, 1)],
                        partner([e]), send_sem.at[c, sem], recv_sem.at[c, sem])
            sem += 1
            yield
            copy.wait()
            acc[pl.ds(mine, 1)] = acc[pl.ds(mine, 1)] + extra_recvs[c][pl.ds(e - SPLIT_BITS, 1)]
        gath[pl.ds(mine, 1)] = encode(acc[pl.ds(mine, 1)] * factor)
        for k in reversed(range(len(order))):
            group, (size, _) = order[k], parts[k]
            span = pl.ds(bases[k + 1], size)
            batch = []
            for chosen in toggles(group):
                batch.append(
                    send(gath.at[span], gath.at[span], partner([group[j] for j in chosen]),
                         send_sem.at[c, sem], recv_sem.at[c, sem])
                )
                sem += 1
            copies.extend(batch)
            yield
            for copy in batch:
                copy.wait_recv()


    running = []

    def advance():
        for chunk in list(running):
            if next(chunk, "end") == "end":
                running.remove(chunk)

    contract_rows = (((0,), (0,)), ((), ()))
    contract_lanes = (((1,), (1,)), ((), ()))
    wide = slcat[...].reshape(bricks * 640, 384)
    for dy in range(3):
        term = lax.dot_general(
            p9[:, :, :, dy * 384 : dy * 384 + 384].reshape(bricks * 640, 384), wide,
            contract_rows, preferred_element_type=F32,
        )
        stacked = jnp.concatenate([term[:, dz * 128 : dz * 128 + 128] for dz in range(3)], axis=0)
        accs[dy][:, :72, :] = stacked.reshape(PIECES, 72, 128)
        if dy == 2:
            term = lax.dot_general(
                up[...].reshape(bricks * 512, 256), slope[...].reshape(bricks * 512, 128),
                contract_rows, preferred_element_type=F32,
            )
            accs[2][:, 72:, :] = term.reshape(PIECES, 16, 128)
        running.append(reduce_chunk(dy))
        next(running[-1])

    for b in range(bricks):
        set_own(b, slope[b].astype(F32).reshape(8, 8, 8, 128))
    for b in range(bricks):
        inner_planes(own, s9, b, index[b])
        advance()
    take_halo(slope_pair, slope_halo)
    for b in range(bricks):
        edge_planes(top, bottom, s9, b, index[b])
    for b in range(bricks):
        total = jnp.zeros((512, 128), F32)
        for dz in range(3):
            total = total + lax.dot_general(
                s9[b, dz : dz + 8].reshape(512, 1152), kt[dz], contract_lanes,
                preferred_element_type=F32,
            )
        gi_out[b] = total.astype(BF16)
        advance()
    while running:
        advance()
    for copy in copies:
        copy.wait_send()


def finish(gi_in, gath_a, gath_b, gath_c, gi_out, gk_out, gc_out, gk, gc, sems):
    first = pltpu.make_async_copy(gi_in, gi_out, sems.at[0])
    first.start()
    copies = [first]
    for c, gath in enumerate((gath_a, gath_b, gath_c)):
        values = decode(gath[...])
        total = values[:, :72, :].reshape(3, 384, 128)
        for dz in range(3):
            gk[dz, c] = total[dz]
        copy = pltpu.make_async_copy(gk.at[:, c], gk_out.at[:, c], sems.at[1 + c])
        copy.start()
        copies.append(copy)
        if c == 2:
            gc[...] = values[:, 72:, :].reshape(256, 128)
    last = pltpu.make_async_copy(gc, gc_out, sems.at[4])
    last.start()
    for copy in copies + [last]:
        copy.wait()


def local(n, features, cotangent, coarse, kernel, coarse_weight, brick_links, parent_slot):
    bricks = features.shape[0]
    bits = n.bit_length() - 1
    factor = (bricks * 512 * n) ** (-0.5)
    heights = (72, 72, 88)
    vmem = pltpu.VMEM
    tall = coarse.shape[0]
    smem = pltpu.SMEM
    scratch = [
        smem(brick_links.shape, jnp.int32),
        smem(parent_slot.shape, jnp.int32),
        vmem((bricks, 512, 128), BF16),
        vmem((bricks, 512, 128), BF16),
        vmem((tall, 8, 64, 256), BF16),
        vmem((3, 1152, 128), BF16),
        vmem((256, 128), BF16),
        pltpu.SemaphoreType.DMA((7,)),
        vmem((bricks + 1, 8, 8, 8, 128), F32),
        vmem((2 * bricks + 1, 8, 8, 128), F32),
        vmem((2 * bricks + 1, 8, 8, 128), F32),
        vmem((2, bricks, 64, 128), BF16),
        vmem((bricks, 512, 128), BF16),
        vmem((2, bricks, 64, 128), BF16),
        vmem((bricks, 10, 64, 1152), BF16),
        vmem((bricks, 10, 64, 1152), BF16),
        vmem((3, 128, 1152), BF16),
        vmem((bricks, 8, 64, 256), BF16),
        vmem((bricks, 10, 64, 384), BF16),
    ]
    short = jnp.int16
    scratch += [vmem((PIECES, h, 128), F32) for h in heights]
    scratch += [vmem((PIECES, h + 8, 128), short) for h in heights]
    for order, h in zip(ORDERS, heights):
        for k, (size, others) in enumerate(stage_parts(order)):
            rows, kind = (h, F32) if k == 0 else (h + 8, short)
            scratch += [vmem((others, size, rows, 128), kind)]
    scratch += [vmem((max(bits - SPLIT_BITS, 1), h, 128), F32) for h in heights]
    steps = 2 * sum(others for _, others in stage_parts(ORDERS[0])) + bits - SPLIT_BITS
    dma = pltpu.SemaphoreType.DMA
    scratch += [dma((3, steps)), dma((3, steps)), dma((2, 2)), dma((2, 2))]
    in_vmem = pl.BlockSpec(memory_space=pltpu.VMEM)
    in_hbm = pl.BlockSpec(memory_space=pltpu.HBM)
    grad, gath_a, gath_b, gath_c = pl.pallas_call(
        functools.partial(body, n, factor),
        out_shape=[jax.ShapeDtypeStruct(features.shape, BF16)]
        + [jax.ShapeDtypeStruct((PIECES, h + 8, 128), short) for h in heights],
        in_specs=[in_hbm] * 7,
        out_specs=[in_vmem] * 4,
        scratch_shapes=scratch,
        compiler_params=pltpu.CompilerParams(
            collective_id=0, has_side_effects=True, vmem_limit_bytes=60 * 1024 * 1024
        ),
        cost_estimate=pl.CostEstimate(flops=3_000_000_000, bytes_accessed=8_000_000, transcendentals=0),
    )(brick_links, parent_slot, features, cotangent,
      coarse.reshape(tall, 8, 64, 256), kernel.reshape(3, 1152, 128), coarse_weight)
    grad, grad_kernel, grad_coarse = pl.pallas_call(
        finish,
        out_shape=(
            jax.ShapeDtypeStruct(features.shape, BF16),
            jax.ShapeDtypeStruct((3, 3, 3 * 128, 128), F32),
            jax.ShapeDtypeStruct((256, 128), F32),
        ),
        in_specs=[in_vmem] * 4,
        out_specs=(in_hbm, in_hbm, in_hbm),
        scratch_shapes=[
            vmem((3, 3, 3 * 128, 128), F32), vmem((256, 128), F32), dma((5,)),
        ],
        compiler_params=pltpu.CompilerParams(vmem_limit_bytes=16 * 1024 * 1024),
    )(grad, gath_a, gath_b, gath_c)
    return grad, grad_kernel.reshape(27, 128, 128), grad_coarse


def solution(mesh):
    return jax.shard_map(
        functools.partial(local, mesh.shape["morton"]),
        mesh=mesh,
        in_specs=(
            P(("groups", "morton"), None, None),
            P(("groups", "morton"), None, None),
            P(("groups", "morton"), None, None),
            P(),
            P(),
            P(("groups", "morton"), None),
            P(("groups", "morton")),
        ),
        out_specs=(P(("groups", "morton"), None, None), P("groups", None, None), P("groups", None)),
        check_vma=False,
    )
```

```python
import functools

import jax
import jax.numpy as jnp
from jax import lax
from jax.experimental import pallas as pl
from jax.experimental.pallas import tpu as pltpu
from jax.sharding import PartitionSpec as P

MESH = pl.DeviceIdType.MESH
F32 = jnp.float32
BF16 = jnp.bfloat16
PIECES = 16
SPLIT_BITS = 4
ORDERS = (((0,), (1,), (2, 3)), ((0,), (2, 3), (1,)), ((0,), (1,), (2, 3)))
LEVELS = 32000.0
TINY = 2.0**-100


def encode(values):
    pieces = values.shape[0]
    peak = jnp.maximum(jnp.max(jnp.abs(values), axis=1, keepdims=True), TINY)
    power = jnp.ceil(jnp.log2(peak))
    scaled = values * (jnp.exp2(-power) * LEVELS)
    both = jnp.concatenate([scaled, jnp.broadcast_to(power, (pieces, 8, 128))], axis=1)
    return jnp.floor(both + 0.5).astype(jnp.int32).astype(jnp.int16)


def decode(codes):
    rows = codes.shape[1] - 8
    both = codes.astype(jnp.int32).astype(F32)
    return both[:, :rows] * (jnp.exp2(both[:, rows : rows + 1]) * (1.0 / LEVELS))


def bit(value, place):
    return (value // (1 << place)) % 2


def stage_parts(order):
    size, parts = PIECES, []
    for group in order:
        size >>= len(group)
        parts.append((size, (1 << len(group)) - 1))
    return parts


def put_plane(rows_of, target, brick, plane):
    columns = [
        jnp.concatenate([rows_of(0, dx), rows_of(1, dx), rows_of(2, dx)], axis=0)
        for dx in range(3)
    ]
    at = lax.broadcasted_iota(jnp.int32, columns[1].shape, 1)
    shifted = (
        pltpu.roll(jnp.where(at == 7, columns[0], columns[1]), 1, 1),
        columns[1],
        pltpu.roll(jnp.where(at == 0, columns[2], columns[1]), 7, 1),
    )
    for dx in range(3):
        flat = shifted[dx].reshape(80, 128)
        for dy in range(3):
            lane = (3 * dy + dx) * 128
            target[brick, plane, :, lane : lane + 128] = flat[8 * dy : 8 * dy + 64].astype(BF16)


ROWS = (slice(7, 8), slice(0, 8), slice(0, 1))


def inner_planes(own, target, brick, index):
    @pl.loop(0, 8)
    def _(z):
        def rows_of(dy, dx):
            return own[index[9 + 3 * dy + dx], z, ROWS[dy]]

        put_plane(rows_of, target, brick, z + 1)


def edge_planes(top, bottom, target, brick, index):
    def rows_top(dy, dx):
        return top[index[3 * dy + dx], ROWS[dy]]

    def rows_bottom(dy, dx):
        return bottom[index[18 + 3 * dy + dx], ROWS[dy]]

    put_plane(rows_top, target, brick, 0)
    put_plane(rows_bottom, target, brick, 9)


def body(n, factor, links_in, parents_in, feat_in, cot_in, coarse_in, kern_in, cweight_in,
         gi_out, gath_a, gath_b, gath_c,
         links, parents, feat, cot, coarse, kern, cweight, load_sem,
         own, top, bottom, halo, slope, slope_halo, p9, s9, kt, up, slcat, *rest):
    accs, codes, gaths = rest[0:3], rest[3:6], (gath_a, gath_b, gath_c)
    stages = len(ORDERS[0])
    recvs = [rest[6 + stages * c : 6 + stages * (c + 1)] for c in range(3)]
    extra_recvs = rest[6 + 3 * stages : 9 + 3 * stages]
    send_sem, recv_sem, halo_send, halo_recv = rest[9 + 3 * stages :]
    bricks = feat.shape[0]
    coarse_bricks = coarse.shape[0]
    me = lax.axis_index("morton")
    group = lax.axis_index("groups")
    after, before = (me + 1) % n, (me + n - 1) % n
    bits = n.bit_length() - 1

    def partner(places):
        other = me
        for b in places:
            other = other + (1 - 2 * bit(me, b)) * (1 << b)
        return other

    def toggles(group):
        return [
            [j for j in range(len(group)) if mask >> j & 1] for mask in range(1, 1 << len(group))
        ]

    partners = [
        partner([group[j] for j in chosen]) for group in ORDERS[0] for chosen in toggles(group)
    ] + [partner([b]) for b in range(SPLIT_BITS, bits)]

    sources = (links_in, parents_in, feat_in, kern_in, coarse_in, cweight_in, cot_in)
    places = (links, parents, feat, kern, coarse, cweight, cot)
    loads = [
        pltpu.make_async_copy(source, place, load_sem.at[i])
        for i, (source, place) in enumerate(zip(sources, places))
    ]
    for load in loads:
        load.start()

    barrier = pltpu.get_barrier_semaphore()
    for other in [after, before] + partners:
        pl.semaphore_signal(barrier, inc=1, device_id=(group, other), device_id_type=MESH)

    def send(source, dest, other, s_sem, r_sem):
        copy = pltpu.make_async_remote_copy(
            src_ref=source, dst_ref=dest, send_sem=s_sem, recv_sem=r_sem,
            device_id=(group, other), device_id_type=MESH,
        )
        copy.start()
        return copy

    copies = []

    def exchange_halo(source, dest, which):
        pair = [
            send(source.at[:, pl.ds(448, 64)], dest.at[0], after,
                 halo_send.at[which, 0], halo_recv.at[which, 0]),
            send(source.at[:, pl.ds(0, 64)], dest.at[1], before,
                 halo_send.at[which, 1], halo_recv.at[which, 1]),
        ]
        copies.extend(pair)
        return pair

    def take_halo(pair, dest):
        for side, copy in enumerate(pair):
            copy.wait_recv()
        for b in range(bricks):
            top[b] = dest[0, b].astype(F32).reshape(8, 8, 128)
            bottom[bricks + b] = dest[1, b].astype(F32).reshape(8, 8, 128)

    def set_own(b, cells):
        own[b] = cells
        top[bricks + b] = cells[7]
        bottom[b] = cells[0]

    for load in loads[:3]:
        load.wait()

    index = []
    for b in range(bricks):
        row = []
        for o in range(27):
            link = links[b, o]
            if o < 9:
                spot, spare = link - (me - 1) * bricks, 2 * bricks
            elif o < 18:
                spot, spare = link - me * bricks, bricks
            else:
                spot, spare = link - me * bricks, 2 * bricks
            row.append(jnp.where(link < 0, spare, jnp.clip(spot, 0, spare)))
        index.append(row)

    own[bricks] = jnp.zeros((8, 8, 8, 128), F32)
    top[2 * bricks] = jnp.zeros((8, 8, 128), F32)
    bottom[2 * bricks] = jnp.zeros((8, 8, 128), F32)
    for b in range(bricks):
        set_own(b, feat[b].astype(F32).reshape(8, 8, 8, 128))
    for b in range(bricks):
        inner_planes(own, p9, b, index[b])
    pl.semaphore_wait(barrier, 2 + len(partners))
    pair = exchange_halo(feat_in, halo, 0)

    for load in loads[3:]:
        load.wait()
    row_at = lax.broadcasted_iota(jnp.int32, (64, 64), 0)
    col_at = lax.broadcasted_iota(jnp.int32, (64, 64), 1)
    for b in range(bricks):
        slot = parents[b]
        octant = slot % 8
        parent = jnp.clip(slot // 8 - me * coarse_bricks, 0, coarse_bricks - 1)
        oz, oy, ox = octant // 4, (octant // 2) % 2, octant % 2
        wanted = (4 * oy + row_at // 16) * 8 + 4 * ox + (row_at % 8) // 2
        pick = jnp.where(col_at == wanted, 1.0, 0.0).astype(BF16)
        for zc in range(4):
            cells = coarse[parent, 4 * oz + zc]
            spread = jnp.dot(pick, cells, preferred_element_type=F32).astype(BF16)
            up[b, 2 * zc] = spread
            up[b, 2 * zc + 1] = spread

    for o in range(27):
        lane = (o % 9) * 128
        mirror = 26 - o
        kt[o // 9, :, lane : lane + 128] = kern[mirror // 9, (mirror % 9) * 128 : (mirror % 9) * 128 + 128, :]

    blank = jnp.zeros((64, 128), BF16)
    for b in range(bricks):
        for dz in range(3):
            for plane in list(range(dz)) + list(range(8 + dz, 10)):
                slcat[b, plane, :, dz * 128 : dz * 128 + 128] = blank

    take_halo(pair, halo)
    for b in range(bricks):
        edge_planes(top, bottom, p9, b, index[b])

    for b in range(bricks):
        total = jnp.dot(up[b].reshape(512, 256), cweight[...], preferred_element_type=F32)
        for dz in range(3):
            total = total + jnp.dot(
                p9[b, dz : dz + 8].reshape(512, 1152), kern[dz], preferred_element_type=F32
            )
        gate = jax.nn.sigmoid(total)
        grads = cot[b].astype(F32)
        value = (grads * gate * (1.0 + total * (1.0 - gate))).astype(BF16)
        slope[b] = value
        for dz in range(3):
            slcat[b, dz : dz + 8, :, dz * 128 : dz * 128 + 128] = value.reshape(8, 64, 128)

    slope_pair = exchange_halo(slope, slope_halo, 1)

    def reduce_chunk(c):
        order = ORDERS[c]
        acc, gath, recv, sem = accs[c], gaths[c], recvs[c], 0
        parts = stage_parts(order)
        digits = [
            sum(bit(me, b) * (1 << (len(group) - 1 - j)) for j, b in enumerate(group)) for group in order
        ]
        bases = [0]
        for digit, (size, _) in zip(digits, parts):
            bases.append(bases[-1] + digit * size)
        filled = 0
        for k, (group, (size, _)) in enumerate(zip(order, parts)):
            batch = []
            for slot, chosen in enumerate(toggles(group)):
                digit = digits[k]
                for j in chosen:
                    digit = digit + (1 - 2 * bit(me, group[j])) * (1 << (len(group) - 1 - j))
                source = acc.at[pl.ds(bases[k] + digit * size, size)]
                if k > 0:
                    coded = codes[c].at[pl.ds(filled, size)]
                    coded[...] = encode(source[...])
                    source = coded
                    filled += size
                batch.append(
                    send(source, recv[k].at[slot], partner([group[j] for j in chosen]),
                         send_sem.at[c, sem], recv_sem.at[c, sem])
                )
                sem += 1
            copies.extend(batch)
            yield
            span = pl.ds(bases[k + 1], size)
            total = acc[span]
            for slot, copy in enumerate(batch):
                copy.wait_recv()
                total = total + (recv[k][slot] if k == 0 else decode(recv[k][slot]))
            acc[span] = total
        mine = bases[-1]
        for e in range(SPLIT_BITS, bits):
            copy = send(acc.at[pl.ds(mine, 1)], extra_recvs[c].at[pl.ds(e - SPLIT_BITS, 1)],
                        partner([e]), send_sem.at[c, sem], recv_sem.at[c, sem])
            sem += 1
            yield
            copy.wait()
            acc[pl.ds(mine, 1)] = acc[pl.ds(mine, 1)] + extra_recvs[c][pl.ds(e - SPLIT_BITS, 1)]
        gath[pl.ds(mine, 1)] = encode(acc[pl.ds(mine, 1)] * factor)
        for k in reversed(range(len(order))):
            group, (size, _) = order[k], parts[k]
            span = pl.ds(bases[k + 1], size)
            batch = []
            for chosen in toggles(group):
                batch.append(
                    send(gath.at[span], gath.at[span], partner([group[j] for j in chosen]),
                         send_sem.at[c, sem], recv_sem.at[c, sem])
                )
                sem += 1
            copies.extend(batch)
            yield
            for copy in batch:
                copy.wait_recv()


    running = []

    def advance():
        for chunk in list(running):
            if next(chunk, "end") == "end":
                running.remove(chunk)

    contract_rows = (((0,), (0,)), ((), ()))
    contract_lanes = (((1,), (1,)), ((), ()))
    wide = slcat[...].reshape(bricks * 640, 384)
    for dy in range(3):
        term = lax.dot_general(
            p9[:, :, :, dy * 384 : dy * 384 + 384].reshape(bricks * 640, 384), wide,
            contract_rows, preferred_element_type=F32,
        )
        stacked = jnp.concatenate([term[:, dz * 128 : dz * 128 + 128] for dz in range(3)], axis=0)
        accs[dy][:, :72, :] = stacked.reshape(PIECES, 72, 128)
        if dy == 2:
            term = lax.dot_general(
                up[...].reshape(bricks * 512, 256), slope[...].reshape(bricks * 512, 128),
                contract_rows, preferred_element_type=F32,
            )
            accs[2][:, 72:, :] = term.reshape(PIECES, 16, 128)
        running.append(reduce_chunk(dy))
        next(running[-1])

    for b in range(bricks):
        set_own(b, slope[b].astype(F32).reshape(8, 8, 8, 128))
    for b in range(bricks):
        inner_planes(own, s9, b, index[b])
        advance()
    take_halo(slope_pair, slope_halo)
    for b in range(bricks):
        edge_planes(top, bottom, s9, b, index[b])
    for b in range(bricks):
        total = jnp.zeros((512, 128), F32)
        for dz in range(3):
            total = total + lax.dot_general(
                s9[b, dz : dz + 8].reshape(512, 1152), kt[dz], contract_lanes,
                preferred_element_type=F32,
            )
        gi_out[b] = total.astype(BF16)
        advance()
    while running:
        advance()
    for copy in copies:
        copy.wait_send()


def finish(gi_in, gath_a, gath_b, gath_c, gi_out, gk_out, gc_out,
           here_gi, here_a, here_b, here_c, gk, gc, load_sems, sems):
    sources, places = (gi_in, gath_a, gath_b, gath_c), (here_gi, here_a, here_b, here_c)
    loads = [
        pltpu.make_async_copy(source, place, load_sems.at[c])
        for c, (source, place) in enumerate(zip(sources, places))
    ]
    for load in loads:
        load.start()
    loads[0].wait()
    first = pltpu.make_async_copy(here_gi, gi_out, sems.at[0])
    first.start()
    copies = [first]
    for c, here in enumerate(places[1:]):
        loads[c + 1].wait()
        values = decode(here[...])
        total = values[:, :72, :].reshape(3, 384, 128)
        for dz in range(3):
            gk[dz, c] = total[dz]
        copy = pltpu.make_async_copy(gk.at[:, c], gk_out.at[:, c], sems.at[1 + c])
        copy.start()
        copies.append(copy)
        if c == 2:
            gc[...] = values[:, 72:, :].reshape(256, 128)
    last = pltpu.make_async_copy(gc, gc_out, sems.at[4])
    last.start()
    for copy in copies + [last]:
        copy.wait()


def local(n, features, cotangent, coarse, kernel, coarse_weight, brick_links, parent_slot):
    bricks = features.shape[0]
    bits = n.bit_length() - 1
    factor = (bricks * 512 * n) ** (-0.5)
    heights = (72, 72, 88)
    vmem = pltpu.VMEM
    tall = coarse.shape[0]
    smem = pltpu.SMEM
    scratch = [
        smem(brick_links.shape, jnp.int32),
        smem(parent_slot.shape, jnp.int32),
        vmem((bricks, 512, 128), BF16),
        vmem((bricks, 512, 128), BF16),
        vmem((tall, 8, 64, 256), BF16),
        vmem((3, 1152, 128), BF16),
        vmem((256, 128), BF16),
        pltpu.SemaphoreType.DMA((7,)),
        vmem((bricks + 1, 8, 8, 8, 128), F32),
        vmem((2 * bricks + 1, 8, 8, 128), F32),
        vmem((2 * bricks + 1, 8, 8, 128), F32),
        vmem((2, bricks, 64, 128), BF16),
        vmem((bricks, 512, 128), BF16),
        vmem((2, bricks, 64, 128), BF16),
        vmem((bricks, 10, 64, 1152), BF16),
        vmem((bricks, 10, 64, 1152), BF16),
        vmem((3, 128, 1152), BF16),
        vmem((bricks, 8, 64, 256), BF16),
        vmem((bricks, 10, 64, 384), BF16),
    ]
    short = jnp.int16
    scratch += [vmem((PIECES, h, 128), F32) for h in heights]
    scratch += [vmem((PIECES, h + 8, 128), short) for h in heights]
    for order, h in zip(ORDERS, heights):
        for k, (size, others) in enumerate(stage_parts(order)):
            rows, kind = (h, F32) if k == 0 else (h + 8, short)
            scratch += [vmem((others, size, rows, 128), kind)]
    scratch += [vmem((max(bits - SPLIT_BITS, 1), h, 128), F32) for h in heights]
    steps = 2 * sum(others for _, others in stage_parts(ORDERS[0])) + bits - SPLIT_BITS
    dma = pltpu.SemaphoreType.DMA
    scratch += [dma((3, steps)), dma((3, steps)), dma((2, 2)), dma((2, 2))]
    in_vmem = pl.BlockSpec(memory_space=pltpu.VMEM)
    in_hbm = pl.BlockSpec(memory_space=pltpu.HBM)
    grad, gath_a, gath_b, gath_c = pl.pallas_call(
        functools.partial(body, n, factor),
        out_shape=[jax.ShapeDtypeStruct(features.shape, BF16)]
        + [jax.ShapeDtypeStruct((PIECES, h + 8, 128), short) for h in heights],
        in_specs=[in_hbm] * 7,
        out_specs=[in_vmem] * 4,
        scratch_shapes=scratch,
        compiler_params=pltpu.CompilerParams(
            collective_id=0, has_side_effects=True, vmem_limit_bytes=60 * 1024 * 1024
        ),
        cost_estimate=pl.CostEstimate(flops=3_000_000_000, bytes_accessed=8_000_000, transcendentals=0),
    )(brick_links, parent_slot, features, cotangent,
      coarse.reshape(tall, 8, 64, 256), kernel.reshape(3, 1152, 128), coarse_weight)
    grad, grad_kernel, grad_coarse = pl.pallas_call(
        finish,
        out_shape=(
            jax.ShapeDtypeStruct(features.shape, BF16),
            jax.ShapeDtypeStruct((3, 3, 3 * 128, 128), F32),
            jax.ShapeDtypeStruct((256, 128), F32),
        ),
        in_specs=[in_hbm] * 4,
        out_specs=(in_hbm, in_hbm, in_hbm),
        scratch_shapes=[
            vmem(features.shape, BF16),
            *[vmem((PIECES, h + 8, 128), short) for h in heights],
            vmem((3, 3, 3 * 128, 128), F32), vmem((256, 128), F32), dma((4,)), dma((5,)),
        ],
        compiler_params=pltpu.CompilerParams(vmem_limit_bytes=60 * 1024 * 1024),
    )(grad, gath_a, gath_b, gath_c)
    return grad, grad_kernel.reshape(27, 128, 128), grad_coarse


def solution(mesh):
    return jax.shard_map(
        functools.partial(local, mesh.shape["morton"]),
        mesh=mesh,
        in_specs=(
            P(("groups", "morton"), None, None),
            P(("groups", "morton"), None, None),
            P(("groups", "morton"), None, None),
            P(),
            P(),
            P(("groups", "morton"), None),
            P(("groups", "morton")),
        ),
        out_specs=(P(("groups", "morton"), None, None), P("groups", None, None), P("groups", None)),
        check_vma=False,
    )
```
